32 devices in a mesh: wide: 16 (over z, y, core), narrow: 2 (over x).
Axes of the slice: x: 2, y: 2, z: 4, core: 2. Of those that a mesh axis runs over, the one named last changes fastest.
Arguments:
- state: bfloat16 [2, 4194304], P(None, ('wide', 'narrow')), may hold values from -6 to 6
- blocks_one: bfloat16 [16, 2, 512, 512], P('wide'), may hold values from -0.1875 to 0.1875
- blocks_two: bfloat16 [16, 2, 512, 512], P('wide'), may hold values from -0.1875 to 0.1875
- control_of: int32 [16], replicated, may hold values from 0 to 15, each once
- ctrl_qubits: int32 [4], replicated, may hold values from 9 to 16, as said below
- angles: float32 [3], replicated, may hold values from -3.140625 to 3.140625
Outputs:
- final_state: float32 [2, 4194304], P(None, ('wide', 'narrow'))
The draws below stay inside these ranges and needn't reach their ends.
Inputs may be any that keep to these rules, and one draw needn't show every extreme that they name: `ctrl_qubits`: distinct local qubits, none of them among the lowest 9; the lowest and the highest allowed qubit are always among them.
All inputs are finite; a program needn't handle non-finite values.
Results may differ from the reference program's by a relative error of at most 0.0041.
Values may be sent and summed in bfloat16 or wider, within the bound.
A program may use at most 64 MiB of HBM per device.

```python
import jax
import jax.numpy as jnp
from jax import lax

LOC = 131072
TGT_BITS = 9
ORDER = 512
LOC_BITS = 17
WBITS = 4
NBITS = 1
BLOCKS = 16
AMPS = 4194304
N_WIDE = 16
N_NARROW = 2


def draw_ctrl_qubits(key, part):
    first_key = jax.random.fold_in(key, 11)
    second_key = jax.random.fold_in(key, 23)
    middle = jax.random.permutation(first_key, LOC_BITS - TGT_BITS - 2) + TGT_BITS + 1
    chosen = jnp.concatenate([jnp.array([TGT_BITS, LOC_BITS - 1], jnp.int32), middle[:WBITS - 2].astype(jnp.int32)])
    order_ids = jax.random.permutation(second_key, WBITS)
    return chosen[order_ids].astype(jnp.int32)


def level_of(own_key, extent, shards, smallest, high):
    loudness, own = 1.0, jax.random.fold_in(own_key, 6)
    for dim, blocks in shards:
        heights = jnp.exp(jax.random.uniform(jax.random.fold_in(own, dim), (blocks,), jnp.float32, smallest / len(shards), high / len(shards)))
        loudness = loudness * jnp.repeat(heights, extent[dim] // blocks).reshape([-1 if axis == dim else 1 for axis in range(len(extent))])
    return loudness


def gaussian(stream_key, dims, scale, limit, shards=(), kind=jnp.bfloat16):
    values = jax.random.normal(stream_key, dims, jnp.float32) * scale
    if len(shards) > 0:
        values = level_of(stream_key, dims, shards, -0.22, 0.18) * values
    return jnp.clip(values, min=-limit, max=limit).astype(kind)


def setup_inputs(seed: int = 0) -> dict:
    seeds = jax.random.split(jax.random.key(seed), 7)
    return {
        "state": gaussian(seeds[0], (2, AMPS), 1.0, 6.0, ((1, 32),)),
        "blocks_one": gaussian(seeds[1], (BLOCKS, 2, ORDER, ORDER), (2 * ORDER) ** -0.5, 0.1875, ((0, 16),)),
        "blocks_two": gaussian(seeds[2], (BLOCKS, 2, ORDER, ORDER), (2 * ORDER) ** -0.5, 0.1875, ((0, 16),)),
        "control_of": jax.random.permutation(seeds[3], BLOCKS).astype(jnp.int32),
        "ctrl_qubits": draw_ctrl_qubits(jax.random.fold_in(seeds[6], 71), 0),
        "angles": jnp.clip(jax.random.uniform(seeds[5], (3,), jnp.float32, -3.140625, 3.140625), -3.140625, 3.140625),
    }


def slot_index(ctrl_qubits, control_of, local_bits, low_count, high_count):
    slot_count = control_of.shape[0]
    qubit_ids = jnp.arange(local_bits, dtype=jnp.int32)
    matches = ctrl_qubits[:, None] == qubit_ids[None, :]
    control_mask = jnp.any(matches, axis=0)
    place_ids = jnp.arange(ctrl_qubits.shape[0], dtype=jnp.int32)
    control_place = jnp.sum(jnp.where(matches, place_ids[:, None], 0), axis=0).astype(jnp.int32)
    rest_rank = (jnp.cumsum(1 - control_mask.astype(jnp.int32)) - 1).astype(jnp.int32)
    values = control_of.astype(jnp.int32).reshape(slot_count, 1, 1)
    low_ids = jnp.arange(low_count, dtype=jnp.int32).reshape(1, low_count, 1)
    high_ids = jnp.arange(high_count, dtype=jnp.int32).reshape(1, 1, high_count)
    rest_index = low_ids + low_count * high_ids
    result = jnp.zeros((slot_count, low_count, high_count), jnp.int32)
    for qubit in range(local_bits):
        from_control = jnp.right_shift(values, control_place[qubit]) & 1
        from_rest = jnp.right_shift(rest_index, jnp.maximum(rest_rank[qubit], 0)) & 1
        chosen_bit = jnp.where(control_mask[qubit], from_control, from_rest)
        result = result + jnp.left_shift(chosen_bit, qubit).astype(jnp.int32)
    return result


def mix_rows(field, weights):
    products = jnp.einsum("crs,dst->cdrt", field.astype(jnp.float32), weights.astype(jnp.float32))
    return jnp.stack([products[0, 0] - products[1, 1], products[0, 1] + products[1, 0]])


def mix_cols(field, weights):
    products = jnp.einsum("cnth,dtu->cdnuh", field.astype(jnp.float32), weights.astype(jnp.float32))
    return jnp.stack([products[0, 0] - products[1, 1], products[0, 1] + products[1, 0]])


def reference(state, blocks_one, blocks_two, control_of, ctrl_qubits, angles):
    low_count = ORDER // N_WIDE
    high_count = LOC // ORDER
    source = state.astype(jnp.float32).reshape(2, N_WIDE, N_NARROW, LOC)

    polar = angles[0] * 0.5
    first_angle = angles[1]
    third_angle = angles[2]
    cosine = jnp.cos(polar)
    sine = jnp.sin(polar)
    top_bit = NBITS - 1
    narrow_ids = jnp.arange(N_NARROW, dtype=jnp.int32)
    own_bit = jnp.right_shift(narrow_ids, top_bit) & 1
    partner_ids = jnp.bitwise_xor(narrow_ids, 2 ** top_bit).astype(jnp.int32)
    partner = jnp.take(source, partner_ids, axis=2)
    upper = own_bit == 1
    own_re = jnp.where(upper, jnp.cos(first_angle + third_angle) * cosine, cosine).reshape(1, N_NARROW, 1)
    own_im = jnp.where(upper, jnp.sin(first_angle + third_angle) * cosine, 0.0).reshape(1, N_NARROW, 1)
    other_re = jnp.where(upper, jnp.cos(first_angle) * sine, -jnp.cos(third_angle) * sine).reshape(1, N_NARROW, 1)
    other_im = jnp.where(upper, jnp.sin(first_angle) * sine, -jnp.sin(third_angle) * sine).reshape(1, N_NARROW, 1)
    new_re = own_re * source[0] - own_im * source[1] + other_re * partner[0] - other_im * partner[1]
    new_im = own_re * source[1] + own_im * source[0] + other_re * partner[1] + other_im * partner[0]
    grid = jnp.stack([new_re, new_im]).astype(jnp.bfloat16)

    def first_gate(index):
        piece = lax.dynamic_index_in_dim(grid, index, 1, keepdims=False)
        rows = piece.reshape(2, N_NARROW * LOC // ORDER, ORDER)
        return mix_rows(rows, blocks_one[index]).astype(jnp.bfloat16).reshape(2, N_NARROW, LOC)

    first = lax.map(first_gate, jnp.arange(N_WIDE, dtype=jnp.int32))
    first = jnp.transpose(first, (1, 0, 2, 3))
    indices = slot_index(ctrl_qubits, control_of, LOC_BITS, low_count, high_count)

    def second_gate(index):
        chosen = jnp.take(first, indices[index].reshape(-1), axis=3)
        chosen = chosen.reshape(2, N_WIDE, N_NARROW, low_count, high_count)
        chosen = jnp.transpose(chosen, (0, 2, 1, 3, 4)).reshape(2, N_NARROW, ORDER, high_count)
        mixed = mix_cols(chosen, blocks_two[index])
        mixed = mixed.reshape(2, N_NARROW, N_WIDE, low_count, high_count)
        return jnp.transpose(mixed, (0, 2, 1, 3, 4)).reshape(2, N_WIDE, N_NARROW, low_count * high_count)

    mixed = lax.map(second_gate, jnp.arange(N_WIDE, dtype=jnp.int32))
    mixed = jnp.transpose(mixed, (1, 2, 3, 0, 4)).reshape(2, N_WIDE, N_NARROW, LOC)
    second = jnp.zeros((2, N_WIDE, N_NARROW, LOC), jnp.float32).at[:, :, :, indices.reshape(-1)].set(mixed)
    return second.reshape(2, N_WIDE * N_NARROW * LOC)
```

```python
import functools

import jax
import jax.numpy as jnp
from jax import lax
from jax.experimental import pallas as pl
from jax.experimental.pallas import tpu as pltpu
from jax.sharding import PartitionSpec as P

LANES = 128
F32 = jnp.float32
BF16 = jnp.bfloat16
MESH = pl.DeviceIdType.MESH


def dot(a, b):
    return jnp.dot(a, b, preferred_element_type=F32)


def slot_and_rank(rows, row_bits, target_bits, ctrl, control_of):
    value = jnp.zeros_like(rows)
    rank = jnp.zeros_like(rows)
    free = jnp.int32(1)
    for bit in range(row_bits):
        here = (rows >> bit) & 1
        weight = jnp.int32(0)
        taken = jnp.int32(0)
        for place, qubit in enumerate(ctrl):
            match = (qubit == bit + target_bits).astype(jnp.int32)
            weight = weight + match * (1 << place)
            taken = taken + match
        value = value + here * weight
        rank = rank + here * (free * (1 - taken))
        free = free * (2 - taken)
    slot = jnp.zeros_like(rows)
    for index, acts_at in enumerate(control_of):
        slot = slot + jnp.where(value == acts_at, index, 0)
    return slot, rank


def coefficients(cosine, sine, upper):
    own_re = jnp.where(upper, cosine[3] * cosine[0], cosine[0])
    own_im = jnp.where(upper, sine[3] * cosine[0], jnp.zeros_like(sine[3]))
    other_re = jnp.where(upper, cosine[1] * sine[0], -cosine[2] * sine[0])
    other_im = jnp.where(upper, sine[1] * sine[0], -sine[2] * sine[0])
    return own_re, own_im, other_re, other_im


def combine(coefs, own_re, own_im, far_re, far_im):
    a, b, c, d = coefs
    return (
        a * own_re - b * own_im + c * far_re - d * far_im,
        a * own_im + b * own_re + c * far_im + d * far_re,
    )


def kernel(
    dims,
    ctrl_ref, cof_ref, ang_ref, x_ref, w1_ref, w2_ref,
    out_ref,
    x32, xs, own, part, rot, wraw, wc1, wc2, perm, back,
    send, recv, xmat, ymat, ysend, ret, rmat,
    load_sem, swap_send, swap_recv, go_send, go_recv, ret_send, ret_recv,
):
    slots, n_narrow, order, rows, phases, low = dims
    slot_rows = rows // slots
    h = slot_rows // phases
    part_rows = rows // phases
    tiles = order // LANES
    group = LANES // low
    v_his = slots // group
    qh = tiles * h
    target_bits = order.bit_length() - 1
    me = lax.axis_index("wide")
    mine = lax.axis_index("narrow")
    partner = lax.rem(mine + n_narrow // 2, n_narrow)

    loads = [
        pltpu.make_async_copy(w_ref.at[0], wraw.at[i], load_sem.at[i])
        for i, w_ref in enumerate((w1_ref, w2_ref))
    ]
    for load in loads:
        load.start()

    barrier = pltpu.get_barrier_semaphore()
    for k in range(1, slots):
        pl.semaphore_signal(barrier, inc=1, device_id=(lax.rem(me + k, slots), mine), device_id_type=MESH)
    pl.semaphore_signal(barrier, inc=1, device_id=(me, partner), device_id_type=MESH)

    x32[...] = x_ref[...].astype(F32)
    for c in range(2):
        for q in range(tiles):
            at = (c * tiles + q) * LANES
            xs[:, at : at + LANES] = x32[pl.ds(q * 2 + c, rows, stride=2 * tiles), :].astype(BF16)

    row_ids = lax.broadcasted_iota(jnp.int32, (8, rows), 1)
    ctrl = [ctrl_ref[i] for i in range(ctrl_ref.shape[0])]
    cof = [cof_ref[i] for i in range(cof_ref.shape[0])]
    slot, rank = slot_and_rank(row_ids, rows.bit_length() - 1, target_bits, ctrl, cof)
    ahead = slot - me
    ahead = jnp.where(ahead < 0, ahead + slots, ahead)
    phase = jnp.zeros_like(rank)
    for i in range(1, phases):
        phase = phase + jnp.where(rank >= i * h, 1, 0)
    dest = phase * part_rows + ahead * h + (rank - phase * h)
    onehot = jnp.where(
        jnp.broadcast_to(dest[0:1, :], (rows, rows)) == lax.broadcasted_iota(jnp.int32, (rows, rows), 0), 1.0, 0.0
    ).astype(F32)
    picked = dot(onehot.astype(BF16), xs[...])
    for ph in range(phases):
        own[ph] = picked[ph * part_rows : (ph + 1) * part_rows, :].astype(BF16)

    pl.semaphore_wait(barrier, slots)

    swaps = []
    for ph in range(phases):
        swap = pltpu.make_async_remote_copy(
            src_ref=own.at[ph], dst_ref=part.at[ph],
            send_sem=swap_send.at[ph], recv_sem=swap_recv.at[ph],
            device_id=(me, partner), device_id_type=MESH,
        )
        swap.start()
        swaps.append(swap)

    back[...] = onehot.T.astype(BF16)
    arg_row = lax.broadcasted_iota(jnp.int32, (8, LANES), 0)
    t, f, g = ang_ref[0], ang_ref[1], ang_ref[2]
    args = jnp.where(arg_row == 0, t * 0.5, jnp.where(arg_row == 1, f, jnp.where(arg_row == 2, g, f + g)))
    cosine, sine = jnp.cos(args), jnp.sin(args)
    upper = mine >= n_narrow // 2
    coefs = coefficients([cosine[i : i + 1] for i in range(4)], [sine[i : i + 1] for i in range(4)], upper)
    for i, wc in enumerate((wc1, wc2)):
        loads[i].wait()
        wc[0:order, 0:order] = wraw[i, 0]
        wc[order:, order:] = wraw[i, 0]
        wc[0:order, order:] = wraw[i, 1]
        wc[order:, 0:order] = -wraw[i, 1]
    span = group * LANES
    p_row = lax.broadcasted_iota(jnp.int32, (span, span), 0)
    p_col = lax.broadcasted_iota(jnp.int32, (span, span), 1)
    turned = (p_row % LANES) // low * LANES + p_row // LANES * low + p_row % low
    perm[...] = jnp.where(turned == p_col, 1.0, 0.0).astype(BF16)

    goes = []
    for ph in range(phases):
        swaps[ph].wait_recv()
        for q in range(tiles):
            re = slice(q * LANES, (q + 1) * LANES)
            im = slice(order + q * LANES, order + (q + 1) * LANES)
            new_re, new_im = combine(
                coefs, own[ph, :, re].astype(F32), own[ph, :, im].astype(F32),
                part[ph, :, re].astype(F32), part[ph, :, im].astype(F32),
            )
            rot[:, re] = new_re.astype(BF16)
            rot[:, im] = new_im.astype(BF16)
        first = dot(rot[...], wc1[...])
        for k in [*range(1, slots), 0]:
            piece = jnp.concatenate(
                [first[k * h : (k + 1) * h, i * LANES : (i + 1) * LANES] for i in range(2 * tiles)], axis=0
            ).astype(BF16)
            if k == 0:
                recv[ph, me] = piece
                continue
            send[ph, k] = piece
            go = pltpu.make_async_remote_copy(
                src_ref=send.at[ph, k], dst_ref=recv.at[ph, me],
                send_sem=go_send.at[ph, k], recv_sem=go_recv.at[ph, k],
                device_id=(lax.rem(me + k, slots), mine), device_id_type=MESH,
            )
            go.start()
            goes.append((ph, go))

    returns = []
    for ph in range(phases):
        for at, go in goes:
            if at == ph:
                go.wait_recv()
        field = jnp.concatenate(
            [
                jnp.concatenate([recv[ph, v_hi * group + v_lo] for v_lo in range(group)], axis=1)
                for v_hi in range(v_his)
            ],
            axis=0,
        )
        turned_in = dot(field, perm[...]).astype(BF16)
        for mid in range(group):
            for c in range(2):
                for v_hi in range(v_his):
                    src = (v_hi * 2 + c) * qh
                    dst = (c * v_his + v_hi) * LANES
                    xmat[mid * qh : (mid + 1) * qh, dst : dst + LANES] = turned_in[
                        src : src + qh, mid * LANES : (mid + 1) * LANES
                    ]
        second = dot(xmat[...], wc2[...]).astype(BF16)
        for mid in range(group):
            for c in range(2):
                for w_hi in range(v_his):
                    dst = (w_hi * 2 + c) * qh
                    src = (c * v_his + w_hi) * LANES
                    ymat[dst : dst + qh, mid * LANES : (mid + 1) * LANES] = second[
                        mid * qh : (mid + 1) * qh, src : src + LANES
                    ]
        turned_out = dot(ymat[...], perm[...]).astype(BF16)
        for w in range(slots):
            w_hi, w_lo = w // group, w % group
            ysend[ph, w] = turned_out[w_hi * 2 * qh : (w_hi + 1) * 2 * qh, w_lo * LANES : (w_lo + 1) * LANES]
        for k in range(1, slots):
            to = lax.rem(me + k, slots)
            go = pltpu.make_async_remote_copy(
                src_ref=ysend.at[ph, to], dst_ref=ret.at[ph, slots - k],
                send_sem=ret_send.at[ph, k], recv_sem=ret_recv.at[ph, k],
                device_id=(to, mine), device_id_type=MESH,
            )
            go.start()
            returns.append((ph, go))
        ret[ph, 0] = ysend[ph, me]

    for ph in range(phases):
        for at, go in returns:
            if at == ph:
                go.wait_recv()
        came = ret[ph].astype(F32).reshape(slots, 2 * tiles, h, LANES)
        for i in range(2 * tiles):
            rmat[ph * part_rows : (ph + 1) * part_rows, i * LANES : (i + 1) * LANES] = (
                came[:, i].reshape(part_rows, LANES).astype(BF16)
            )
    final = dot(back[...], rmat[...])
    for c in range(2):
        for q in range(tiles):
            at = (c * tiles + q) * LANES
            out_ref[pl.ds(q * 2 + c, rows, stride=2 * tiles), :] = final[:, at : at + LANES]

    for swap in swaps:
        swap.wait_send()
    for _, go in goes + returns:
        go.wait_send()


def fused(dims, state, blocks_one, blocks_two, control_of, ctrl_qubits, angles):
    slots, n_narrow, order, rows, phases, low = dims
    tiles = order // LANES
    slot_rows = rows // slots
    h = slot_rows // phases
    part_rows = rows // phases
    group = LANES // low
    span = group * LANES
    piece = 2 * tiles * h
    lines = rows * tiles
    x = state.reshape(2, lines, LANES).transpose(1, 0, 2).reshape(2 * lines, LANES)
    smem = pl.BlockSpec(memory_space=pltpu.SMEM)
    vmem = pl.BlockSpec(memory_space=pltpu.VMEM)
    hbm = pl.BlockSpec(memory_space=pl.ANY)
    dma = pltpu.SemaphoreType.DMA
    out = pl.pallas_call(
        functools.partial(kernel, dims),
        out_shape=jax.ShapeDtypeStruct((2 * lines, LANES), F32),
        in_specs=[smem, smem, smem, vmem, hbm, hbm],
        out_specs=vmem,
        scratch_shapes=[
            pltpu.VMEM((2 * lines, LANES), F32),
            pltpu.VMEM((rows, 2 * order), BF16),
            pltpu.VMEM((phases, part_rows, 2 * order), BF16),
            pltpu.VMEM((phases, part_rows, 2 * order), BF16),
            pltpu.VMEM((part_rows, 2 * order), BF16),
            pltpu.VMEM((2, 2, order, order), BF16),
            pltpu.VMEM((2 * order, 2 * order), BF16),
            pltpu.VMEM((2 * order, 2 * order), BF16),
            pltpu.VMEM((span, span), BF16),
            pltpu.VMEM((rows, rows), BF16),
            pltpu.VMEM((phases, slots, piece, LANES), BF16),
            pltpu.VMEM((phases, slots, piece, LANES), BF16),
            pltpu.VMEM((group * tiles * h, 2 * order), BF16),
            pltpu.VMEM((slots // group * piece, span), BF16),
            pltpu.VMEM((phases, slots, piece, LANES), BF16),
            pltpu.VMEM((phases, slots, piece, LANES), BF16),
            pltpu.VMEM((rows, 2 * order), BF16),
            dma((2,)),
            dma((phases,)),
            dma((phases,)),
            dma((phases, slots)),
            dma((phases, slots)),
            dma((phases, slots)),
            dma((phases, slots)),
        ],
        compiler_params=pltpu.CompilerParams(
            collective_id=0, has_side_effects=True, vmem_limit_bytes=40 * 2**20
        ),
    )(ctrl_qubits, control_of, angles, x, blocks_one, blocks_two)
    return out.reshape(lines, 2, LANES).transpose(1, 0, 2).reshape(2, lines * LANES)


def complex_dot(spec, field, weights):
    products = jnp.einsum(spec, field, weights, preferred_element_type=F32)
    return jnp.stack([products[0, 0] - products[1, 1], products[0, 1] + products[1, 0]])


def plain(dims, state, blocks_one, blocks_two, control_of, ctrl_qubits, angles):
    slots, n_narrow, order, rows, _, low = dims
    slot_rows = rows // slots
    mids = order // low
    mine = lax.axis_index("narrow")
    half = n_narrow // 2
    pairs = [(source, (source + half) % n_narrow) for source in range(n_narrow)]
    far = lax.ppermute(state, "narrow", pairs).astype(F32)
    near = state.astype(F32)
    args = [angles[0] * 0.5, angles[1], angles[2], angles[1] + angles[2]]
    coefs = coefficients([jnp.cos(a) for a in args], [jnp.sin(a) for a in args], mine >= half)
    rotated = jnp.stack(combine(coefs, near[0], near[1], far[0], far[1])).astype(BF16)
    row_ids = jnp.arange(rows, dtype=jnp.int32)
    ctrl = [ctrl_qubits[i] for i in range(ctrl_qubits.shape[0])]
    cof = [control_of[i] for i in range(control_of.shape[0])]
    slot, rank = slot_and_rank(row_ids, rows.bit_length() - 1, order.bit_length() - 1, ctrl, cof)
    dest = slot * slot_rows + rank
    onehot = (dest[None, :] == row_ids[:, None]).astype(BF16)
    first = complex_dot("crs,dst->cdrt", rotated.reshape(2, rows, order), blocks_one[0]).astype(BF16)
    picked = jnp.einsum("pr,crt->cpt", onehot, first, preferred_element_type=F32).astype(BF16)
    picked = picked.reshape(2, slots, slot_rows, mids, low)
    arranged = jnp.transpose(picked, (0, 1, 4, 2, 3)).reshape(2, slots, low, rows)
    received = lax.all_to_all(arranged, "wide", split_axis=1, concat_axis=2, tiled=True)
    mixed = complex_dot("cth,dtu->cduh", received[:, 0], blocks_two[0]).astype(BF16)[:, None]
    returned = lax.all_to_all(mixed, "wide", split_axis=2, concat_axis=1, tiled=True)
    returned = returned.reshape(2, slots, low, slot_rows, mids)
    returned = jnp.transpose(returned, (0, 1, 3, 4, 2)).reshape(2, rows, order)
    final = jnp.einsum("pr,cpt->crt", onehot, returned, preferred_element_type=F32)
    return final.reshape(2, rows * order)


def shards(*operands):
    state, blocks_one = operands[:2]
    slots = lax.axis_size("wide")
    order = blocks_one.shape[2]
    rows = state.shape[1] // order
    low = order // slots
    slot_rows = rows // slots
    phases = 2 if slot_rows % 16 == 0 else 1
    dims = (slots, lax.axis_size("narrow"), order, rows, phases, low)
    fits = slot_rows % 8 == 0 and LANES % low == 0 and slots % (LANES // low) == 0
    return (fused if fits else plain)(dims, *operands)


def solution(mesh):
    in_specs = (
        P(None, ("wide", "narrow")),
        P("wide", None, None, None),
        P("wide", None, None, None),
        P(),
        P(),
        P(),
    )
    out_specs = P(None, ("wide", "narrow"))
    return jax.shard_map(shards, mesh=mesh, in_specs=in_specs, out_specs=out_specs, check_vma=False)
```

```python
import functools

import jax
import jax.numpy as jnp
from jax import lax
from jax.experimental import pallas as pl
from jax.experimental.pallas import tpu as pltpu
from jax.sharding import PartitionSpec as P

LANES = 128
LANE_BITS = 7
CUTS = 4
F32 = jnp.float32
BF16 = jnp.bfloat16
MESH = pl.DeviceIdType.MESH


def dot(a, b):
    return jnp.dot(a, b, preferred_element_type=F32)


def slot_and_rank(rows, row_bits, target_bits, ctrl, control_of):
    value = jnp.zeros_like(rows)
    rank = jnp.zeros_like(rows)
    free = jnp.int32(1)
    for bit in range(row_bits):
        here = (rows >> bit) & 1
        weight = jnp.int32(0)
        taken = jnp.int32(0)
        for place, qubit in enumerate(ctrl):
            match = (qubit == bit + target_bits).astype(jnp.int32)
            weight = weight + match * (1 << place)
            taken = taken + match
        value = value + here * weight
        rank = rank + here * (free * (1 - taken))
        free = free * (2 - taken)
    slot = jnp.zeros_like(rows)
    for index, acts_at in enumerate(control_of):
        slot = slot + jnp.where(value == acts_at, index, 0)
    return slot, rank


def visit_order(slots):
    half = slots // 2
    return [half + i // 2 if i % 2 == 0 else half - 1 - i // 2 for i in range(slots)]


def coefficients(cosine, sine, upper):
    own_re = jnp.where(upper, cosine[3] * cosine[0], cosine[0])
    own_im = jnp.where(upper, sine[3] * cosine[0], jnp.zeros_like(sine[3]))
    other_re = jnp.where(upper, cosine[1] * sine[0], -cosine[2] * sine[0])
    other_im = jnp.where(upper, sine[1] * sine[0], -sine[2] * sine[0])
    return own_re, own_im, other_re, other_im


def combine(coefs, own_re, own_im, far_re, far_im):
    a, b, c, d = coefs
    return (
        a * own_re - b * own_im + c * far_re - d * far_im,
        a * own_im + b * own_re + c * far_im + d * far_re,
    )


def kernel(
    dims,
    ctrl_ref, cof_ref, ang_ref, x_ref, w1_ref, w2_ref,
    out_ref,
    xraw, x32, xs, own, part, rot, wraw, wc1, wc2, perm, back,
    send, recv, xmat, ymat, ysend, ret, rmat,
    load_sem, swap_send, swap_recv, go_send, go_recv, ret_send, ret_recv,
):
    slots, n_narrow, order, rows, phases, low = dims
    slot_rows = rows // slots
    h = slot_rows // phases
    part_rows = rows // phases
    tiles = order // LANES
    group = LANES // low
    v_his = slots // group
    qh = tiles * h
    target_bits = order.bit_length() - 1
    me = lax.axis_index("wide")
    mine = lax.axis_index("narrow")
    order_of = visit_order(slots)
    partner = lax.rem(mine + n_narrow // 2, n_narrow)

    loads = [
        pltpu.make_async_copy(w_ref.at[0], wraw.at[i], load_sem.at[i])
        for i, w_ref in enumerate((w1_ref, w2_ref))
    ]
    fetch = pltpu.make_async_copy(x_ref, xraw, load_sem.at[2])
    for load in [fetch, *loads]:
        load.start()

    barrier = pltpu.get_barrier_semaphore()
    for k in range(1, slots):
        pl.semaphore_signal(barrier, inc=1, device_id=(lax.rem(me + k, slots), mine), device_id_type=MESH)
    pl.semaphore_signal(barrier, inc=1, device_id=(me, partner), device_id_type=MESH)

    fetch.wait()
    x32[...] = xraw[...].astype(F32)
    for c in range(2):
        for q in range(tiles):
            at = (c * tiles + q) * LANES
            xs[:, at : at + LANES] = x32[pl.ds(q * 2 + c, rows, stride=2 * tiles), :].astype(BF16)

    row_ids = lax.broadcasted_iota(jnp.int32, (8, rows), 1)
    ctrl = [ctrl_ref[i] for i in range(ctrl_ref.shape[0])]
    cof = [cof_ref[i] for i in range(cof_ref.shape[0])]
    slot, rank = slot_and_rank(row_ids, rows.bit_length() - 1, target_bits, ctrl, cof)
    ahead = slot - me
    ahead = jnp.where(ahead < 0, ahead + slots, ahead)
    phase = jnp.zeros_like(rank)
    for i in range(1, phases):
        phase = phase + jnp.where(rank >= i * h, 1, 0)
    half = slots // 2
    place = jnp.where(ahead >= half, 2 * (ahead - half), 2 * (half - ahead) - 1)
    dest = phase * part_rows + place * h + (rank - phase * h)
    onehot = jnp.where(
        jnp.broadcast_to(dest[0:1, :], (rows, rows)) == lax.broadcasted_iota(jnp.int32, (rows, rows), 0), 1.0, 0.0
    ).astype(F32)
    picked = dot(onehot.astype(BF16), xs[...])
    for ph in range(phases):
        for cut in range(own.shape[1]):
            at = (ph * own.shape[1] + cut) * own.shape[2]
            own[ph, cut] = picked[at : at + own.shape[2], :].astype(BF16)

    pl.semaphore_wait(barrier, slots)

    cuts = CUTS
    per_cut = slots // cuts
    swaps = []
    for ph in range(phases):
        for cut in range(cuts):
            swap = pltpu.make_async_remote_copy(
                src_ref=own.at[ph, cut], dst_ref=part.at[ph, cut],
                send_sem=swap_send.at[ph, cut], recv_sem=swap_recv.at[ph, cut],
                device_id=(me, partner), device_id_type=MESH,
            )
            swap.start()
            swaps.append(swap)

    back[...] = onehot.T.astype(BF16)
    arg_row = lax.broadcasted_iota(jnp.int32, (8, LANES), 0)
    t, f, g = ang_ref[0], ang_ref[1], ang_ref[2]
    args = jnp.where(arg_row == 0, t * 0.5, jnp.where(arg_row == 1, f, jnp.where(arg_row == 2, g, f + g)))
    cosine, sine = jnp.cos(args), jnp.sin(args)
    upper = mine >= n_narrow // 2
    coefs = coefficients([cosine[i : i + 1] for i in range(4)], [sine[i : i + 1] for i in range(4)], upper)
    for i, wc in enumerate((wc1, wc2)):
        loads[i].wait()
        wc[0:order, 0:order] = wraw[i, 0]
        wc[order:, order:] = wraw[i, 0]
        wc[0:order, order:] = wraw[i, 1]
        wc[order:, 0:order] = -wraw[i, 1]
    span = group * LANES
    p_row = lax.broadcasted_iota(jnp.int32, (span, span), 0)
    p_col = lax.broadcasted_iota(jnp.int32, (span, span), 1)
    low_bits = low.bit_length() - 1
    turned = ((p_row & (LANES - 1)) >> low_bits) * LANES + (p_row >> LANE_BITS) * low + (p_row & (low - 1))
    perm[...] = jnp.where(turned == p_col, 1.0, 0.0).astype(BF16)

    goes = []
    for ph in range(phases):
        for cut in range(cuts):
            swaps[ph * cuts + cut].wait_recv()
            for q in range(tiles):
                re = slice(q * LANES, (q + 1) * LANES)
                im = slice(order + q * LANES, order + (q + 1) * LANES)
                new_re, new_im = combine(
                    coefs, own[ph, cut, :, re].astype(F32), own[ph, cut, :, im].astype(F32),
                    part[ph, cut, :, re].astype(F32), part[ph, cut, :, im].astype(F32),
                )
                rot[:, re] = new_re.astype(BF16)
                rot[:, im] = new_im.astype(BF16)
            first = dot(rot[...], wc1[...])
            for i in range(per_cut):
                k = order_of[cut * per_cut + i]
                piece = jnp.concatenate(
                    [first[i * h : (i + 1) * h, j * LANES : (j + 1) * LANES] for j in range(2 * tiles)], axis=0
                ).astype(BF16)
                if k == 0:
                    recv[ph, me] = piece
                    continue
                send[ph, k] = piece
                go = pltpu.make_async_remote_copy(
                    src_ref=send.at[ph, k], dst_ref=recv.at[ph, me],
                    send_sem=go_send.at[ph, k], recv_sem=go_recv.at[ph, k],
                    device_id=(lax.rem(me + k, slots), mine), device_id_type=MESH,
                )
                go.start()
                goes.append((ph, go))

    returns = []
    for ph in range(phases):
        for at, go in goes:
            if at == ph:
                go.wait_recv()
        field = jnp.concatenate(
            [
                jnp.concatenate([recv[ph, v_hi * group + v_lo] for v_lo in range(group)], axis=1)
                for v_hi in range(v_his)
            ],
            axis=0,
        )
        turned_in = dot(field, perm[...]).astype(BF16)
        for mid in range(group):
            for c in range(2):
                for v_hi in range(v_his):
                    src = (v_hi * 2 + c) * qh
                    dst = (c * v_his + v_hi) * LANES
                    xmat[mid * qh : (mid + 1) * qh, dst : dst + LANES] = turned_in[
                        src : src + qh, mid * LANES : (mid + 1) * LANES
                    ]
        second = dot(xmat[...], wc2[...]).astype(BF16)
        for mid in range(group):
            for c in range(2):
                for w_hi in range(v_his):
                    dst = (w_hi * 2 + c) * qh
                    src = (c * v_his + w_hi) * LANES
                    ymat[dst : dst + qh, mid * LANES : (mid + 1) * LANES] = second[
                        mid * qh : (mid + 1) * qh, src : src + LANES
                    ]
        turned_out = dot(ymat[...], perm[...]).astype(BF16)
        for w in range(slots):
            w_hi, w_lo = w // group, w % group
            ysend[ph, w] = turned_out[w_hi * 2 * qh : (w_hi + 1) * 2 * qh, w_lo * LANES : (w_lo + 1) * LANES]
        for k in order_of[:-1]:
            to = lax.rem(me + k, slots)
            go = pltpu.make_async_remote_copy(
                src_ref=ysend.at[ph, to], dst_ref=ret.at[ph, order_of.index(slots - k)],
                send_sem=ret_send.at[ph, k], recv_sem=ret_recv.at[ph, k],
                device_id=(to, mine), device_id_type=MESH,
            )
            go.start()
            returns.append((ph, go))
        ret[ph, slots - 1] = ysend[ph, me]

    final = None
    for ph in range(phases):
        for at, go in returns:
            if at == ph:
                go.wait_recv()
        came = ret[ph].astype(F32).reshape(slots, 2 * tiles, h, LANES)
        for i in range(2 * tiles):
            rmat[:, i * LANES : (i + 1) * LANES] = came[:, i].reshape(part_rows, LANES).astype(BF16)
        add = dot(back[:, ph * part_rows : (ph + 1) * part_rows], rmat[...])
        final = add if final is None else final + add
    for c in range(2):
        for q in range(tiles):
            at = (c * tiles + q) * LANES
            out_ref[pl.ds(q * 2 + c, rows, stride=2 * tiles), :] = final[:, at : at + LANES]

    for swap in swaps:
        swap.wait_send()
    for _, go in goes + returns:
        go.wait_send()


def fused(dims, state, blocks_one, blocks_two, control_of, ctrl_qubits, angles):
    slots, n_narrow, order, rows, phases, low = dims
    tiles = order // LANES
    slot_rows = rows // slots
    h = slot_rows // phases
    part_rows = rows // phases
    group = LANES // low
    span = group * LANES
    piece = 2 * tiles * h
    cuts = CUTS
    lines = rows * tiles
    x = state.reshape(2, lines, LANES).transpose(1, 0, 2).reshape(2 * lines, LANES)
    smem = pl.BlockSpec(memory_space=pltpu.SMEM)
    vmem = pl.BlockSpec(memory_space=pltpu.VMEM)
    hbm = pl.BlockSpec(memory_space=pl.ANY)
    dma = pltpu.SemaphoreType.DMA
    out = pl.pallas_call(
        functools.partial(kernel, dims),
        out_shape=jax.ShapeDtypeStruct((2 * lines, LANES), F32),
        in_specs=[smem, smem, smem, hbm, hbm, hbm],
        out_specs=vmem,
        scratch_shapes=[
            pltpu.VMEM((2 * lines, LANES), BF16),
            pltpu.VMEM((2 * lines, LANES), F32),
            pltpu.VMEM((rows, 2 * order), BF16),
            pltpu.VMEM((phases, cuts, part_rows // cuts, 2 * order), BF16),
            pltpu.VMEM((phases, cuts, part_rows // cuts, 2 * order), BF16),
            pltpu.VMEM((part_rows // cuts, 2 * order), BF16),
            pltpu.VMEM((2, 2, order, order), BF16),
            pltpu.VMEM((2 * order, 2 * order), BF16),
            pltpu.VMEM((2 * order, 2 * order), BF16),
            pltpu.VMEM((span, span), BF16),
            pltpu.VMEM((rows, rows), BF16),
            pltpu.VMEM((phases, slots, piece, LANES), BF16),
            pltpu.VMEM((phases, slots, piece, LANES), BF16),
            pltpu.VMEM((group * tiles * h, 2 * order), BF16),
            pltpu.VMEM((slots // group * piece, span), BF16),
            pltpu.VMEM((phases, slots, piece, LANES), BF16),
            pltpu.VMEM((phases, slots, piece, LANES), BF16),
            pltpu.VMEM((part_rows, 2 * order), BF16),
            dma((3,)),
            dma((phases, cuts)),
            dma((phases, cuts)),
            dma((phases, slots)),
            dma((phases, slots)),
            dma((phases, slots)),
            dma((phases, slots)),
        ],
        compiler_params=pltpu.CompilerParams(
            collective_id=0, has_side_effects=True, vmem_limit_bytes=60 * 2**20
        ),
    )(ctrl_qubits, control_of, angles, x, blocks_one, blocks_two)
    return out.reshape(lines, 2, LANES).transpose(1, 0, 2).reshape(2, lines * LANES)


def complex_dot(spec, field, weights):
    products = jnp.einsum(spec, field, weights, preferred_element_type=F32)
    return jnp.stack([products[0, 0] - products[1, 1], products[0, 1] + products[1, 0]])


def plain(dims, state, blocks_one, blocks_two, control_of, ctrl_qubits, angles):
    slots, n_narrow, order, rows, _, low = dims
    slot_rows = rows // slots
    mids = order // low
    mine = lax.axis_index("narrow")
    half = n_narrow // 2
    pairs = [(source, (source + half) % n_narrow) for source in range(n_narrow)]
    far = lax.ppermute(state, "narrow", pairs).astype(F32)
    near = state.astype(F32)
    args = [angles[0] * 0.5, angles[1], angles[2], angles[1] + angles[2]]
    coefs = coefficients([jnp.cos(a) for a in args], [jnp.sin(a) for a in args], mine >= half)
    rotated = jnp.stack(combine(coefs, near[0], near[1], far[0], far[1])).astype(BF16)
    row_ids = jnp.arange(rows, dtype=jnp.int32)
    ctrl = [ctrl_qubits[i] for i in range(ctrl_qubits.shape[0])]
    cof = [control_of[i] for i in range(control_of.shape[0])]
    slot, rank = slot_and_rank(row_ids, rows.bit_length() - 1, order.bit_length() - 1, ctrl, cof)
    dest = slot * slot_rows + rank
    onehot = (dest[None, :] == row_ids[:, None]).astype(BF16)
    first = complex_dot("crs,dst->cdrt", rotated.reshape(2, rows, order), blocks_one[0]).astype(BF16)
    picked = jnp.einsum("pr,crt->cpt", onehot, first, preferred_element_type=F32).astype(BF16)
    picked = picked.reshape(2, slots, slot_rows, mids, low)
    arranged = jnp.transpose(picked, (0, 1, 4, 2, 3)).reshape(2, slots, low, rows)
    received = lax.all_to_all(arranged, "wide", split_axis=1, concat_axis=2, tiled=True)
    mixed = complex_dot("cth,dtu->cduh", received[:, 0], blocks_two[0]).astype(BF16)[:, None]
    returned = lax.all_to_all(mixed, "wide", split_axis=2, concat_axis=1, tiled=True)
    returned = returned.reshape(2, slots, low, slot_rows, mids)
    returned = jnp.transpose(returned, (0, 1, 3, 4, 2)).reshape(2, rows, order)
    final = jnp.einsum("pr,cpt->crt", onehot, returned, preferred_element_type=F32)
    return final.reshape(2, rows * order)


def shards(*operands):
    state, blocks_one = operands[:2]
    slots = lax.axis_size("wide")
    order = blocks_one.shape[2]
    rows = state.shape[1] // order
    low = order // slots
    slot_rows = rows // slots
    phases = 2 if slot_rows % 16 == 0 else 1
    dims = (slots, lax.axis_size("narrow"), order, rows, phases, low)
    fits = slot_rows % 8 == 0 and slots % CUTS == 0 and LANES % low == 0 and slots % (LANES // low) == 0
    return (fused if fits else plain)(dims, *operands)


def solution(mesh):
    in_specs = (
        P(None, ("wide", "narrow")),
        P("wide", None, None, None),
        P("wide", None, None, None),
        P(),
        P(),
        P(),
    )
    out_specs = P(None, ("wide", "narrow"))
    return jax.shard_map(shards, mesh=mesh, in_specs=in_specs, out_specs=out_specs, check_vma=False)
```

```python
import functools

import jax
import jax.numpy as jnp
from jax import lax
from jax.experimental import pallas as pl
from jax.experimental.pallas import tpu as pltpu
from jax.sharding import PartitionSpec as P

LANES = 128
LANE_BITS = 7
CUTS = 4
F32 = jnp.float32
BF16 = jnp.bfloat16
MESH = pl.DeviceIdType.MESH


def dot(a, b):
    return jnp.dot(a, b, preferred_element_type=F32)


def slot_and_rank(rows, row_bits, target_bits, ctrl, control_of):
    value = jnp.zeros_like(rows)
    rank = jnp.zeros_like(rows)
    free = jnp.int32(1)
    for bit in range(row_bits):
        here = (rows >> bit) & 1
        weight = jnp.int32(0)
        taken = jnp.int32(0)
        for place, qubit in enumerate(ctrl):
            match = (qubit == bit + target_bits).astype(jnp.int32)
            weight = weight + match * (1 << place)
            taken = taken + match
        value = value + here * weight
        rank = rank + here * (free * (1 - taken))
        free = free * (2 - taken)
    slot = jnp.zeros_like(rows)
    for index, acts_at in enumerate(control_of):
        slot = slot + jnp.where(value == acts_at, index, 0)
    return slot, rank


def visit_order(slots):
    half = slots // 2
    return [half + i // 2 if i % 2 == 0 else half - 1 - i // 2 for i in range(slots)]


def coefficients(cosine, sine, upper):
    own_re = jnp.where(upper, cosine[3] * cosine[0], cosine[0])
    own_im = jnp.where(upper, sine[3] * cosine[0], jnp.zeros_like(sine[3]))
    other_re = jnp.where(upper, cosine[1] * sine[0], -cosine[2] * sine[0])
    other_im = jnp.where(upper, sine[1] * sine[0], -sine[2] * sine[0])
    return own_re, own_im, other_re, other_im


def combine(coefs, own_re, own_im, far_re, far_im):
    a, b, c, d = coefs
    return (
        a * own_re - b * own_im + c * far_re - d * far_im,
        a * own_im + b * own_re + c * far_im + d * far_re,
    )


def kernel(
    dims,
    ctrl_ref, cof_ref, ang_ref, x_ref, w1_ref, w2_ref,
    out_ref,
    xraw, x32, xs, own, part, rot, wraw, wc1, wc2, perm, back,
    send, recv, xmat, ymat, ysend, ret, rmat,
    load_sem, swap_send, swap_recv, go_send, go_recv, ret_send, ret_recv,
):
    slots, n_narrow, order, rows, phases, low = dims
    slot_rows = rows // slots
    h = slot_rows // phases
    part_rows = rows // phases
    tiles = order // LANES
    group = LANES // low
    v_his = slots // group
    qh = tiles * h
    target_bits = order.bit_length() - 1
    me = lax.axis_index("wide")
    mine = lax.axis_index("narrow")
    order_of = visit_order(slots)
    partner = lax.rem(mine + n_narrow // 2, n_narrow)

    loads = [
        pltpu.make_async_copy(w_ref.at[0], wraw.at[i], load_sem.at[i])
        for i, w_ref in enumerate((w1_ref, w2_ref))
    ]
    fetch = pltpu.make_async_copy(x_ref, xraw, load_sem.at[2])
    for load in [fetch, *loads]:
        load.start()

    barrier = pltpu.get_barrier_semaphore()
    for k in range(1, slots):
        pl.semaphore_signal(barrier, inc=1, device_id=(lax.rem(me + k, slots), mine), device_id_type=MESH)
    pl.semaphore_signal(barrier, inc=1, device_id=(me, partner), device_id_type=MESH)

    fetch.wait()
    x32[...] = xraw[...].astype(F32)
    for c in range(2):
        for q in range(tiles):
            at = (c * tiles + q) * LANES
            xs[:, at : at + LANES] = x32[pl.ds(q * 2 + c, rows, stride=2 * tiles), :].astype(BF16)

    row_ids = lax.broadcasted_iota(jnp.int32, (8, rows), 1)
    ctrl = [ctrl_ref[i] for i in range(ctrl_ref.shape[0])]
    cof = [cof_ref[i] for i in range(cof_ref.shape[0])]
    slot, rank = slot_and_rank(row_ids, rows.bit_length() - 1, target_bits, ctrl, cof)
    ahead = slot - me
    ahead = jnp.where(ahead < 0, ahead + slots, ahead)
    phase = jnp.zeros_like(rank)
    for i in range(1, phases):
        phase = phase + jnp.where(rank >= i * h, 1, 0)
    half = slots // 2
    place = jnp.where(ahead >= half, 2 * (ahead - half), 2 * (half - ahead) - 1)
    dest = phase * part_rows + place * h + (rank - phase * h)
    onehot = jnp.where(
        jnp.broadcast_to(dest[0:1, :], (rows, rows)) == lax.broadcasted_iota(jnp.int32, (rows, rows), 0), 1.0, 0.0
    ).astype(F32)
    picked = dot(onehot.astype(BF16), xs[...])
    for ph in range(phases):
        for cut in range(own.shape[1]):
            at = (ph * own.shape[1] + cut) * own.shape[2]
            own[ph, cut] = picked[at : at + own.shape[2], :].astype(BF16)

    pl.semaphore_wait(barrier, slots)

    cuts = CUTS
    per_cut = slots // cuts
    swaps = []
    for ph in range(phases):
        for cut in range(cuts):
            swap = pltpu.make_async_remote_copy(
                src_ref=own.at[ph, cut], dst_ref=part.at[ph, cut],
                send_sem=swap_send.at[ph, cut], recv_sem=swap_recv.at[ph, cut],
                device_id=(me, partner), device_id_type=MESH,
            )
            swap.start()
            swaps.append(swap)

    back[...] = onehot.T.astype(BF16)
    arg_row = lax.broadcasted_iota(jnp.int32, (8, LANES), 0)
    t, f, g = ang_ref[0], ang_ref[1], ang_ref[2]
    args = jnp.where(arg_row == 0, t * 0.5, jnp.where(arg_row == 1, f, jnp.where(arg_row == 2, g, f + g)))
    cosine, sine = jnp.cos(args), jnp.sin(args)
    upper = mine >= n_narrow // 2
    coefs = coefficients([cosine[i : i + 1] for i in range(4)], [sine[i : i + 1] for i in range(4)], upper)
    for i, wc in enumerate((wc1, wc2)):
        loads[i].wait()
        wc[0:order, 0:order] = wraw[i, 0]
        wc[order:, order:] = wraw[i, 0]
        wc[0:order, order:] = wraw[i, 1]
        wc[order:, 0:order] = -wraw[i, 1]
    span = group * LANES
    p_row = lax.broadcasted_iota(jnp.int32, (span, span), 0)
    p_col = lax.broadcasted_iota(jnp.int32, (span, span), 1)
    low_bits = low.bit_length() - 1
    turned = ((p_row & (LANES - 1)) >> low_bits) * LANES + (p_row >> LANE_BITS) * low + (p_row & (low - 1))
    perm[...] = jnp.where(turned == p_col, 1.0, 0.0).astype(BF16)

    goes = []
    for ph in range(phases):
        for cut in range(cuts):
            swaps[ph * cuts + cut].wait_recv()
            for q in range(tiles):
                re = slice(q * LANES, (q + 1) * LANES)
                im = slice(order + q * LANES, order + (q + 1) * LANES)
                new_re, new_im = combine(
                    coefs, own[ph, cut, :, re].astype(F32), own[ph, cut, :, im].astype(F32),
                    part[ph, cut, :, re].astype(F32), part[ph, cut, :, im].astype(F32),
                )
                rot[:, re] = new_re.astype(BF16)
                rot[:, im] = new_im.astype(BF16)
            first = dot(rot[...], wc1[...])
            for i in range(per_cut):
                k = order_of[cut * per_cut + i]
                piece = jnp.concatenate(
                    [first[i * h : (i + 1) * h, j * LANES : (j + 1) * LANES] for j in range(2 * tiles)], axis=0
                ).astype(BF16)
                if k == 0:
                    recv[ph, me] = piece
                    continue
                send[ph, k] = piece
                go = pltpu.make_async_remote_copy(
                    src_ref=send.at[ph, k], dst_ref=recv.at[ph, me],
                    send_sem=go_send.at[ph, k], recv_sem=go_recv.at[ph, k],
                    device_id=(lax.rem(me + k, slots), mine), device_id_type=MESH,
                )
                go.start()
                goes.append((ph, go))

    returns = []
    for ph in range(phases):
        for at, go in goes:
            if at == ph:
                go.wait_recv()
        field = jnp.concatenate(
            [
                jnp.concatenate([recv[ph, v_hi * group + v_lo] for v_lo in range(group)], axis=1)
                for v_hi in range(v_his)
            ],
            axis=0,
        )
        turned_in = dot(field, perm[...]).astype(BF16)
        for mid in range(group):
            for c in range(2):
                for v_hi in range(v_his):
                    src = (v_hi * 2 + c) * qh
                    dst = (c * v_his + v_hi) * LANES
                    xmat[mid * qh : (mid + 1) * qh, dst : dst + LANES] = turned_in[
                        src : src + qh, mid * LANES : (mid + 1) * LANES
                    ]
        second = dot(xmat[...], wc2[...]).astype(BF16)
        for mid in range(group):
            for c in range(2):
                for w_hi in range(v_his):
                    dst = (w_hi * 2 + c) * qh
                    src = (c * v_his + w_hi) * LANES
                    ymat[dst : dst + qh, mid * LANES : (mid + 1) * LANES] = second[
                        mid * qh : (mid + 1) * qh, src : src + LANES
                    ]
        turned_out = dot(ymat[...], perm[...]).astype(BF16)
        for w in range(slots):
            w_hi, w_lo = w // group, w % group
            ysend[ph, w] = turned_out[w_hi * 2 * qh : (w_hi + 1) * 2 * qh, w_lo * LANES : (w_lo + 1) * LANES]
        for k in order_of[:-1]:
            to = lax.rem(me + k, slots)
            go = pltpu.make_async_remote_copy(
                src_ref=ysend.at[ph, to], dst_ref=ret.at[ph, order_of.index(slots - k)],
                send_sem=ret_send.at[ph, k], recv_sem=ret_recv.at[ph, k],
                device_id=(to, mine), device_id_type=MESH,
            )
            go.start()
            returns.append((ph, go))
        ret[ph, slots - 1] = ysend[ph, me]

    final = None
    for ph in range(phases):
        for at, go in returns:
            if at == ph:
                go.wait_recv()
        came = ret[ph].astype(F32).reshape(slots, 2 * tiles, h, LANES)
        for i in range(2 * tiles):
            rmat[:, i * LANES : (i + 1) * LANES] = came[:, i].reshape(part_rows, LANES).astype(BF16)
        add = dot(back[:, ph * part_rows : (ph + 1) * part_rows], rmat[...])
        final = add if final is None else final + add
    for c in range(2):
        for q in range(tiles):
            at = (c * tiles + q) * LANES
            out_ref[pl.ds(q * 2 + c, rows, stride=2 * tiles), :] = final[:, at : at + LANES]

    for swap in swaps:
        swap.wait_send()
    for _, go in goes + returns:
        go.wait_send()


def fused(dims, state, blocks_one, blocks_two, control_of, ctrl_qubits, angles):
    slots, n_narrow, order, rows, phases, low = dims
    tiles = order // LANES
    slot_rows = rows // slots
    h = slot_rows // phases
    part_rows = rows // phases
    group = LANES // low
    span = group * LANES
    piece = 2 * tiles * h
    cuts = CUTS
    lines = rows * tiles
    x = state.reshape(2, lines, LANES).transpose(1, 0, 2).reshape(2 * lines, LANES)
    smem = pl.BlockSpec(memory_space=pltpu.SMEM)
    vmem = pl.BlockSpec(memory_space=pltpu.VMEM)
    hbm = pl.BlockSpec(memory_space=pl.ANY)
    dma = pltpu.SemaphoreType.DMA
    out = pl.pallas_call(
        functools.partial(kernel, dims),
        out_shape=jax.ShapeDtypeStruct((2 * lines, LANES), F32),
        in_specs=[smem, smem, smem, hbm, hbm, hbm],
        out_specs=vmem,
        scratch_shapes=[
            pltpu.VMEM((2 * lines, LANES), BF16),
            pltpu.VMEM((2 * lines, LANES), F32),
            pltpu.VMEM((rows, 2 * order), BF16),
            pltpu.VMEM((phases, cuts, part_rows // cuts, 2 * order), BF16),
            pltpu.VMEM((phases, cuts, part_rows // cuts, 2 * order), BF16),
            pltpu.VMEM((part_rows // cuts, 2 * order), BF16),
            pltpu.VMEM((2, 2, order, order), BF16),
            pltpu.VMEM((2 * order, 2 * order), BF16),
            pltpu.VMEM((2 * order, 2 * order), BF16),
            pltpu.VMEM((span, span), BF16),
            pltpu.VMEM((rows, rows), BF16),
            pltpu.VMEM((phases, slots, piece, LANES), BF16),
            pltpu.VMEM((phases, slots, piece, LANES), BF16),
            pltpu.VMEM((group * tiles * h, 2 * order), BF16),
            pltpu.VMEM((slots // group * piece, span), BF16),
            pltpu.VMEM((phases, slots, piece, LANES), BF16),
            pltpu.VMEM((phases, slots, piece, LANES), BF16),
            pltpu.VMEM((part_rows, 2 * order), BF16),
            dma((3,)),
            dma((phases, cuts)),
            dma((phases, cuts)),
            dma((phases, slots)),
            dma((phases, slots)),
            dma((phases, slots)),
            dma((phases, slots)),
        ],
        compiler_params=pltpu.CompilerParams(
            collective_id=0, has_side_effects=True, vmem_limit_bytes=52 * 2**20
        ),
    )(ctrl_qubits, control_of, angles, x, blocks_one, blocks_two)
    return out.reshape(lines, 2, LANES).transpose(1, 0, 2).reshape(2, lines * LANES)


def complex_dot(spec, field, weights):
    products = jnp.einsum(spec, field, weights, preferred_element_type=F32)
    return jnp.stack([products[0, 0] - products[1, 1], products[0, 1] + products[1, 0]])


def plain(dims, state, blocks_one, blocks_two, control_of, ctrl_qubits, angles):
    slots, n_narrow, order, rows, _, low = dims
    slot_rows = rows // slots
    mids = order // low
    mine = lax.axis_index("narrow")
    half = n_narrow // 2
    pairs = [(source, (source + half) % n_narrow) for source in range(n_narrow)]
    far = lax.ppermute(state, "narrow", pairs).astype(F32)
    near = state.astype(F32)
    args = [angles[0] * 0.5, angles[1], angles[2], angles[1] + angles[2]]
    coefs = coefficients([jnp.cos(a) for a in args], [jnp.sin(a) for a in args], mine >= half)
    rotated = jnp.stack(combine(coefs, near[0], near[1], far[0], far[1])).astype(BF16)
    row_ids = jnp.arange(rows, dtype=jnp.int32)
    ctrl = [ctrl_qubits[i] for i in range(ctrl_qubits.shape[0])]
    cof = [control_of[i] for i in range(control_of.shape[0])]
    slot, rank = slot_and_rank(row_ids, rows.bit_length() - 1, order.bit_length() - 1, ctrl, cof)
    dest = slot * slot_rows + rank
    onehot = (dest[None, :] == row_ids[:, None]).astype(BF16)
    first = complex_dot("crs,dst->cdrt", rotated.reshape(2, rows, order), blocks_one[0]).astype(BF16)
    picked = jnp.einsum("pr,crt->cpt", onehot, first, preferred_element_type=F32).astype(BF16)
    picked = picked.reshape(2, slots, slot_rows, mids, low)
    arranged = jnp.transpose(picked, (0, 1, 4, 2, 3)).reshape(2, slots, low, rows)
    received = lax.all_to_all(arranged, "wide", split_axis=1, concat_axis=2, tiled=True)
    mixed = complex_dot("cth,dtu->cduh", received[:, 0], blocks_two[0]).astype(BF16)[:, None]
    returned = lax.all_to_all(mixed, "wide", split_axis=2, concat_axis=1, tiled=True)
    returned = returned.reshape(2, slots, low, slot_rows, mids)
    returned = jnp.transpose(returned, (0, 1, 3, 4, 2)).reshape(2, rows, order)
    final = jnp.einsum("pr,cpt->crt", onehot, returned, preferred_element_type=F32)
    return final.reshape(2, rows * order)


def shards(*operands):
    state, blocks_one = operands[:2]
    slots = lax.axis_size("wide")
    order = blocks_one.shape[2]
    rows = state.shape[1] // order
    low = order // slots
    slot_rows = rows // slots
    phases = 2 if slot_rows % 16 == 0 else 1
    dims = (slots, lax.axis_size("narrow"), order, rows, phases, low)
    fits = slot_rows % 8 == 0 and slots % CUTS == 0 and LANES % low == 0 and slots % (LANES // low) == 0
    return (fused if fits else plain)(dims, *operands)


def solution(mesh):
    in_specs = (
        P(None, ("wide", "narrow")),
        P("wide", None, None, None),
        P("wide", None, None, None),
        P(),
        P(),
        P(),
    )
    out_specs = P(None, ("wide", "narrow"))
    return jax.shard_map(shards, mesh=mesh, in_specs=in_specs, out_specs=out_specs, check_vma=False)
```
